256 devices in a mesh: row: 16 (over z, x_hi), rep: 16 (over x_lo, y, core).
Axes of the slice: x: 4 (x_hi: 2, x_lo: 2; x = x_hi * 2 + x_lo), y: 4, z: 8, core: 2. Of those that a mesh axis runs over, the one named last changes fastest.
Arguments:
- grad_out: bfloat16 [65536, 512], P(('row', 'rep')), may hold values from -6 to 6
- relu_mask: int32 [65536, 512], P(('row', 'rep')), may hold values 0 or 1
- aggregated: bfloat16 [65536, 512], P(('row', 'rep')), may hold values from -0.059814453 to 0.059814453
- weight: bfloat16 [512, 512], replicated, may hold values from -0.25 to 0.25
- tile_values: bfloat16 [16, 16, 4, 24, 128, 128], P('row', 'rep'), may hold values from 0 to 0.099609375
- tile_src: int32 [16, 16, 4, 24], P('row', 'rep'), may hold values from 0 to 1, as said below
- tile_dst: int32 [16, 16, 4, 24], P('row', 'rep'), may hold values from 0 to 31
- tile_count: int32 [16, 16, 4], P('row', 'rep'), may hold values from 3 to 24, as said below
Outputs:
- input_grad: bfloat16 [65536, 512], P(('row', 'rep'))
- weight_grad: float32 [512, 512], replicated
The draws below stay inside these ranges and needn't reach their ends.
Inputs may be any that keep to these rules, and one draw needn't show every extreme that they name: `tile_src`: in each list no pair of source and destination block repeats, slots past the count included. `tile_count`: some list is full in every draw.
All inputs are finite; a program needn't handle non-finite values. No bound on the sum of `relu_mask` on one device may be relied on, other than what follows from the above.
Results may differ from the reference program's by a relative error of at most 0.018.
Values may be sent and summed in bfloat16 or wider, within the bound.
No kernel may reach another device: no remote copies, remote signals or barrier semaphores. Data moves between devices by JAX's collectives and lax.ppermute only.
A program may use at most 128 MiB of HBM per device.

```python
import jax
import jax.numpy as jnp
from jax import lax

F = 512
BLOCK = 128
BLK_DEV = 2
SECTIONS = 4
TILES = 24
NODES = 65536
RGROUPS = 16
REPLICAS = 16


def permuted_pairs(pair_key):
    return jax.random.permutation(pair_key, BLK_DEV * RGROUPS * BLK_DEV)[:TILES]


def tile_pairs(key):
    lists = RGROUPS * REPLICAS * SECTIONS
    keys = jax.random.split(key, lists)
    picked = jax.vmap(permuted_pairs)(keys)
    return picked.reshape(RGROUPS, REPLICAS, SECTIONS, TILES).astype(jnp.int32)


def draw_tile_src(key, part):
    return (tile_pairs(key) // (RGROUPS * BLK_DEV)).astype(jnp.int32)


def draw_tile_dst(key, part):
    return (tile_pairs(key) % (RGROUPS * BLK_DEV)).astype(jnp.int32)


def draw_tile_count(key, part):
    key = jax.random.fold_in(key, 7)
    base_key, full_key, spot_key = jax.random.split(key, 3)
    shape = (RGROUPS, REPLICAS, SECTIONS)
    base = jax.random.randint(base_key, shape, max(1, TILES // 8), TILES // 2 + 1).astype(jnp.int32)
    chosen = jax.random.randint(full_key, shape, 0, 8) == 0
    counts = jnp.where(chosen, TILES, base).reshape(-1)
    lists = RGROUPS * REPLICAS * SECTIONS
    spot = jax.random.randint(spot_key, (), 0, lists)
    counts = jnp.where(jnp.arange(lists, dtype=jnp.int32) == spot, TILES, counts)
    return counts.reshape(shape).astype(jnp.int32)


def place_ends(drawn, stream_key, least, largest):
    dims = drawn.shape
    place = [jax.random.randint(jax.random.fold_in(stream_key, axis), (), 0, dims[axis]) for axis in range(len(dims))]
    drawn = drawn.at[tuple(place)].set(least)
    longest = dims.index(max(dims))
    place[longest] = (place[longest] + 1) % dims[longest]
    return drawn.at[tuple(place)].set(largest)


def block_levels(key, extent, pieces, smallest, largest):
    level = 1.0
    for axis_at, blocks in pieces:
        steps = jax.random.uniform(jax.random.fold_in(jax.random.fold_in(key, 6), axis_at), (blocks,), jnp.float32, smallest / len(pieces), largest / len(pieces))
        level = level * jnp.repeat(jnp.exp(steps), extent[axis_at] // blocks).reshape((-1,) + (1,) * (len(extent) - 1 - axis_at))
    return level


def bell_draw(rng, shape, scale, bound, cuts=(), kind=jnp.bfloat16):
    loudness = block_levels(rng, shape, cuts, -0.22, 0.18) if cuts else 1.0
    entries = jax.random.normal(rng, shape, jnp.float32) * scale * loudness
    return jnp.minimum(jnp.maximum(entries, -bound), bound).astype(kind)


def setup_inputs(seed: int = 0) -> dict:
    key_of = jax.random.split(jax.random.key(seed), 9)
    grad_out = bell_draw(key_of[0], (NODES, F), 1.0, 6.0, ((0, 256),))
    relu_mask = place_ends((jax.random.randint(key_of[1], (NODES, F), 0, 2) < 1).astype(jnp.int32), jax.random.fold_in(key_of[1], 1), 0, 1)
    aggregated = bell_draw(key_of[2], (NODES, F), 0.01, 0.059814453, ((0, 256),))
    weight = bell_draw(key_of[3], (F, F), F ** -0.5, 0.25)
    tile_values = jnp.clip(0.099609375 * jax.random.uniform(key_of[4], (RGROUPS, REPLICAS, SECTIONS, TILES, BLOCK, BLOCK), jnp.float32) ** block_levels(key_of[4], (RGROUPS, REPLICAS, SECTIONS, TILES, BLOCK, BLOCK), ((0, 16), (1, 16)), -0.2, 0.2), 0.0, 0.099609375).astype(jnp.bfloat16)
    tile_src = draw_tile_src(jax.random.fold_in(key_of[8], 71), 0)
    tile_dst = draw_tile_dst(jax.random.fold_in(key_of[8], 71), 0)
    tile_count = draw_tile_count(jax.random.fold_in(key_of[8], 71), 0)
    return dict(grad_out=grad_out, relu_mask=relu_mask, aggregated=aggregated, weight=weight, tile_values=tile_values, tile_src=tile_src, tile_dst=tile_dst, tile_count=tile_count)


def reference(grad_out, relu_mask, aggregated, weight, tile_values, tile_src, tile_dst, tile_count):
    masked = jnp.where(relu_mask != 0, grad_out, jnp.zeros_like(grad_out))
    node_grad = lax.dot_general(masked, weight, (((1,), (1,)), ((), ())), preferred_element_type=jnp.float32).astype(jnp.bfloat16)
    weight_grad = lax.dot_general(aggregated, masked, (((0,), (0,)), ((), ())), preferred_element_type=jnp.float32)
    groups = tile_src.shape[0]
    replicas = tile_src.shape[1]
    slab_blocks = groups * BLK_DEV
    owner_blocks = node_grad.reshape(groups, replicas, BLK_DEV, BLOCK, F)
    slot_index = jnp.arange(TILES, dtype=jnp.int32)

    def one_device(totals, device_index):
        group_index = device_index // replicas
        rep_index = device_index % replicas
        partial_value = jnp.zeros((slab_blocks, BLOCK, F), jnp.float32)
        for section_index in range(SECTIONS):
            source = owner_blocks[group_index, section_index]
            tile_vals = tile_values[group_index, rep_index, section_index].astype(jnp.float32)
            gathered = source[tile_src[group_index, rep_index, section_index]].astype(jnp.float32)
            products = jnp.einsum("tab,taf->tbf", tile_vals, gathered, precision=lax.Precision.HIGHEST)
            alive = (slot_index < tile_count[group_index, rep_index, section_index]).astype(jnp.float32)
            partial_value = partial_value.at[tile_dst[group_index, rep_index, section_index]].add(products * alive[:, None, None])
        sent = lax.optimization_barrier(partial_value.astype(jnp.bfloat16)).astype(jnp.float32)
        current = lax.dynamic_index_in_dim(totals, rep_index, 0, False)
        totals = lax.dynamic_update_index_in_dim(totals, current + sent, rep_index, 0)
        return totals, None

    totals = jnp.zeros((replicas, slab_blocks, BLOCK, F), jnp.float32)
    totals, _ = lax.scan(one_device, totals, jnp.arange(groups * replicas, dtype=jnp.int32))
    arranged = totals.reshape(replicas, groups, BLK_DEV * BLOCK, F).transpose(1, 0, 2, 3)
    input_grad = arranged.reshape(groups * replicas * BLK_DEV * BLOCK, F).astype(jnp.bfloat16)
    return input_grad, weight_grad
```

```python
import jax
import jax.numpy as jnp
from jax import lax
from jax.experimental import pallas as pl
from jax.experimental.pallas import tpu as pltpu
from jax.sharding import PartitionSpec as P

AXES = ("row", "rep")
X, Y, Z, C = 4, 4, 8, 2


def index_of(x, y, z, c):
    return (z * 2 + x // 2) * 16 + (x % 2) * 8 + y * 2 + c


def pairs(move):
    out = []
    for z in range(Z):
        for x in range(X):
            for y in range(Y):
                for c in range(C):
                    to = move(x, y, z, c)
                    if to is not None:
                        out.append((index_of(x, y, z, c), index_of(to[0] % X, to[1] % Y, to[2] % Z, to[3] % C)))
    return out


def send(value, move):
    return lax.ppermute(value, AXES, pairs(move))


def add(*terms):
    total = terms[0].astype(jnp.float32)
    for term in terms[1:]:
        total = total + term.astype(jnp.float32)
    return total


def narrow(value):
    return value.astype(jnp.bfloat16)


def flood(block, x_lo, y):
    def across(x, y, z, c):
        return (x + 1, y, z, c) if x % 2 == 0 and y < 2 else None

    def outward(x, y, z, c):
        return (x, 3 - y, z, c) if x % 2 == 0 and y < 2 else None

    def swap(x, y, z, c):
        return (x, 1 - y, z, c) if x % 2 == 0 and y < 2 else None

    by_x = send(block, across)
    by_y = send(block, outward)
    swapped = send(block, swap)
    first = jnp.where(x_lo == 0, jnp.where(y < 2, block, by_y), by_x)

    def swap_rest(x, y, z, c):
        if x % 2 == 0 and y >= 2:
            return (x, 5 - y, z, c)
        if x % 2 == 1 and y < 2:
            return (x, 1 - y, z, c)
        return None

    def across_rest(x, y, z, c):
        return (x + 1, y, z, c) if x % 2 == 0 and y >= 2 else None

    def far(x, y, z, c):
        return (x, y + 2, z, c) if x % 2 == 1 and y < 2 else None

    second = send(first, swap_rest)
    by_x2 = send(first, across_rest)
    by_y2 = send(first, far)
    last = jnp.logical_and(x_lo == 1, y >= 2)
    first = jnp.where(last, by_x2, first)
    second = jnp.where(last, by_y2, jnp.where(jnp.logical_and(x_lo == 0, y < 2), swapped, second))
    flip = jnp.logical_or(y == 1, y == 2)
    even = jnp.where(flip, second, first)
    odd = jnp.where(flip, first, second)
    return even, odd


def tiles_kernel(src_ref, dst_ref, count_ref, place_ref, tiles_ref, a_ref, b_ref, c_ref, d_ref, *rest):
    outs, (acc, held) = rest[:16], rest[16:]
    z, xh, core = place_ref[0], place_ref[1], place_ref[2]
    acc[...] = jnp.zeros_like(acc)
    for i, ref in enumerate((a_ref, b_ref, c_ref, d_ref)):
        held[2 * i] = ref[:128, :]
        held[2 * i + 1] = ref[128:, :]
    for section in range(4):
        slot = jnp.where(core == section % 2, section // 2, 2 + section // 2)

        def step(t, carry):
            d = dst_ref[section, t]
            s = src_ref[section, t]
            rel = lax.rem(d // 4 - z + 8, 8)
            half = lax.rem(d // 2 + xh, 2)
            at = rel * 4 + half * 2 + lax.rem(d, 2)
            product = lax.dot_general(
                tiles_ref[section * 24 + t],
                held[slot * 2 + s],
                (((0,), (0,)), ((), ())),
                preferred_element_type=jnp.float32,
            )
            acc[at] += product
            return carry

        lax.fori_loop(0, count_ref[section], step, 0)
    for i in range(16):
        for j in range(2):
            outs[i][pl.ds(j * 128, 128), :] = acc[2 * i + j].astype(jnp.bfloat16)


def tile_partials(src, dst, count, place, tiles, sources):
    smem = pl.BlockSpec(memory_space=pltpu.SMEM)
    vmem = pl.BlockSpec(memory_space=pltpu.VMEM)
    return pl.pallas_call(
        tiles_kernel,
        out_shape=[jax.ShapeDtypeStruct((256, 512), jnp.bfloat16)] * 16,
        in_specs=[smem] * 4 + [vmem] * 5,
        out_specs=[vmem] * 16,
        scratch_shapes=[pltpu.VMEM((32, 128, 512), jnp.float32), pltpu.VMEM((8, 128, 512), jnp.bfloat16)],
        compiler_params=pltpu.CompilerParams(vmem_limit_bytes=48 * 1024 * 1024),
        name="tile_partials",
    )(src, dst, count, place, tiles, *sources)


def up(x, y, z, c):
    return (x, y, z + 1, c)


def down(x, y, z, c):
    return (x, y, z - 1, c)


def chain(first, terms, move):
    moving = first
    for term in terms:
        moving = narrow(add(send(moving, move), term))
    return send(moving, move)


def spread(value, size, me, hop):
    rows = value.shape[0] // size
    own = lax.dynamic_slice_in_dim(value, me * rows, rows, 0)
    parts = [own]
    for k in range(1, size):
        to = lax.rem(me + k, size)
        piece = narrow(lax.dynamic_slice_in_dim(value, to * rows, rows, 0))
        parts.append(send(piece, hop(k)))
    return add(*parts)


def collect(value, size, me, hop):
    rows = value.shape[0]
    out = jnp.zeros((size, rows, value.shape[1]), value.dtype)
    out = lax.dynamic_update_slice_in_dim(out, value[None], me, 0)
    for k in range(1, size):
        got = send(value, hop(k))
        out = lax.dynamic_update_slice_in_dim(out, got[None], lax.rem(me - k + size, size), 0)
    return out.reshape(size * rows, value.shape[1])


HOPS = {
    "c": lambda k: lambda x, y, z, c: (x, y, z, c + k),
    "y": lambda k: lambda x, y, z, c: (x, y + k, z, c),
    "x": lambda k: lambda x, y, z, c: (x + k, y, z, c),
    "z": lambda k: lambda x, y, z, c: (x, y, z + k, c),
}


def local(grad_out, relu_mask, aggregated, weight, tile_values, tile_src, tile_dst, tile_count):
    row, rep = lax.axis_index("row"), lax.axis_index("rep")
    z, x_hi = row // 2, row % 2
    x_lo, y, core = rep // 8, (rep // 2) % 4, rep % 2
    masked = jnp.where(relu_mask != 0, grad_out, jnp.zeros_like(grad_out))
    node_grad = lax.dot_general(
        masked, weight, (((1,), (1,)), ((), ())), preferred_element_type=jnp.float32
    ).astype(jnp.bfloat16)
    even, odd = flood(node_grad, x_lo, y)
    other = HOPS["c"](1)
    sources = (even, odd, send(even, other), send(odd, other))
    place = jnp.stack([z, x_hi, core]).astype(jnp.int32)
    tiles = tile_values.reshape(tile_values.shape[2] * tile_values.shape[3], 128, 128)
    parts = tile_partials(tile_src[0, 0], tile_dst[0, 0], tile_count[0, 0], place, tiles, sources)
    mine = [parts[2 * k] for k in range(8)]
    theirs = [parts[2 * k + 1] for k in range(8)]
    theirs_up = chain(theirs[4], [theirs[3], theirs[2], theirs[1]], up)
    theirs_down = chain(theirs[5], [theirs[6], theirs[7]], down)
    crossing = narrow(add(theirs[0], theirs_up, theirs_down))
    crossed = send(crossing, HOPS["x"](2))
    mine_down = chain(mine[4], [mine[5], mine[6], mine[7]], down)
    mine_up = chain(mine[3], [mine[2], mine[1]], up)
    input_grad = narrow(add(mine[0], mine_up, mine_down, crossed))

    local_wgrad = lax.dot_general(
        aggregated, masked, (((0,), (0,)), ((), ())), preferred_element_type=jnp.float32
    )
    x = x_hi * 2 + x_lo
    total = spread(local_wgrad, C, core, HOPS["c"])
    total = spread(total, Y, y, HOPS["y"])
    total = spread(total, X, x, HOPS["x"])
    total = spread(total, Z, z, HOPS["z"])
    total = narrow(total)
    total = collect(total, Z, z, HOPS["z"])
    total = collect(total, X, x, HOPS["x"])
    total = collect(total, Y, y, HOPS["y"])
    total = collect(total, C, core, HOPS["c"])
    return (input_grad, total.astype(jnp.float32))


def solution(mesh):
    in_specs = (
        P(("row", "rep"), None),
        P(("row", "rep"), None),
        P(("row", "rep"), None),
        P(),
        P("row", "rep", None, None, None, None),
        P("row", "rep", None, None),
        P("row", "rep", None, None),
        P("row", "rep", None),
    )
    out_specs = (P(("row", "rep"), None), P())
    return jax.shard_map(local, mesh=mesh, in_specs=in_specs, out_specs=out_specs, check_vma=False)
```

```python
import functools

import jax
import jax.numpy as jnp
from jax import lax
from jax.experimental import pallas as pl
from jax.experimental.pallas import tpu as pltpu
from jax.sharding import PartitionSpec as P

AXES = ("row", "rep")
X, Y, Z, C = 4, 4, 8, 2


def index_of(x, y, z, c):
    return (z * 2 + x // 2) * 16 + (x % 2) * 8 + y * 2 + c


def pairs(move):
    out = []
    for z in range(Z):
        for x in range(X):
            for y in range(Y):
                for c in range(C):
                    to = move(x, y, z, c)
                    if to is not None:
                        out.append((index_of(x, y, z, c), index_of(to[0] % X, to[1] % Y, to[2] % Z, to[3] % C)))
    return out


def send(value, move):
    return lax.ppermute(value, AXES, pairs(move))


def add(*terms):
    total = terms[0].astype(jnp.float32)
    for term in terms[1:]:
        total = total + term.astype(jnp.float32)
    return total


def narrow(value):
    return value.astype(jnp.bfloat16)


def flood(block, x_lo, y):
    def across(x, y, z, c):
        return (x + 1, y, z, c) if x % 2 == 0 and y < 2 else None

    def outward(x, y, z, c):
        return (x, 3 - y, z, c) if x % 2 == 0 and y < 2 else None

    def swap(x, y, z, c):
        return (x, 1 - y, z, c) if x % 2 == 0 and y < 2 else None

    by_x = send(block, across)
    by_y = send(block, outward)
    swapped = send(block, swap)

    def swap_rest(x, y, z, c):
        return (x, 5 - y, z, c) if x % 2 == 0 and y >= 2 else None

    def across_all(x, y, z, c):
        return (x + 1, y, z, c) if x % 2 == 0 else None

    def distant(x, y, z, c):
        return (x, y + 2, z, c) if x % 2 == 1 and y < 2 else None

    by_far = send(by_x, distant)
    by_swap = send(by_y, swap_rest)
    by_x2 = send(jnp.where(y < 2, swapped, by_y), across_all)
    first = jnp.where(x_lo == 0, jnp.where(y < 2, block, by_y), jnp.where(y < 2, by_x, by_x2))
    second = jnp.where(x_lo == 0, jnp.where(y < 2, swapped, by_swap), jnp.where(y < 2, by_x2, by_far))
    flip = jnp.logical_or(y == 1, y == 2)
    even = jnp.where(flip, second, first)
    odd = jnp.where(flip, first, second)
    return even, odd


FIRST = [(4, 1), (3, 1), (5, 1)]
SECOND = [(4, 0), (2, 1), (6, 1), (3, 0), (5, 0), (1, 1), (7, 1), (2, 0), (6, 0), (0, 1), (1, 0), (7, 0), (0, 0)]
SLOTS = 96


def plan_kernel(src_ref, dst_ref, count_ref, place_ref, order_ref, list_ref, filled_ref):
    z, xh, core = place_ref[0], place_ref[1], place_ref[2]
    for i in range(32):
        filled_ref[i] = 0
    for section in range(4):
        slot = jnp.where(core == section % 2, section // 2, 2 + section // 2)

        def step(t, carry):
            d = dst_ref[section, t]
            s = src_ref[section, t]
            rel = lax.rem(d // 4 - z + 8, 8)
            half = lax.rem(d // 2 + xh, 2)
            at = order_ref[rel * 2 + half] * 2 + lax.rem(d, 2)
            n = filled_ref[at]
            list_ref[at, n] = (section * 24 + t) * 8 + slot * 2 + s
            filled_ref[at] = n + 1
            return carry

        lax.fori_loop(0, count_ref[section], step, 0)


def plan(src, dst, count, place):
    order = [0] * 16
    for i, (rel, half) in enumerate(FIRST + SECOND):
        order[rel * 2 + half] = i
    smem = pl.BlockSpec(memory_space=pltpu.SMEM)
    return pl.pallas_call(
        plan_kernel,
        out_shape=[
            jax.ShapeDtypeStruct((32, 8), jnp.int32),
            jax.ShapeDtypeStruct((32,), jnp.int32),
        ],
        in_specs=[smem] * 5,
        out_specs=[smem, smem],
        name="plan",
    )(src, dst, count, place, jnp.array(order, jnp.int32))


def rows_kernel(base, groups, list_ref, filled_ref, tiles_ref, sources_ref, *rest):
    outs, acc = rest[:groups], rest[groups]

    def pair(at, p, n):
        one = list_ref[at, 2 * p]
        paired = 2 * p + 1 < n
        two = jnp.where(paired, list_ref[at, 2 * p + 1], 0)
        second = tiles_ref[two // 8]
        left = jnp.concatenate([tiles_ref[one // 8], jnp.where(paired, second, jnp.zeros_like(second))], axis=0)
        right = jnp.concatenate([sources_ref[lax.rem(one, 8)], sources_ref[lax.rem(two, 8)]], axis=0)
        return lax.dot_general(left, right, (((0,), (0,)), ((), ())), preferred_element_type=jnp.float32)

    for g in range(groups):
        def block(j, carry):
            at = base + 2 * g + j
            n = filled_ref[at]
            out = outs[g].at[pl.ds(pl.multiple_of(j * 128, 128), 128), :]

            @pl.when(n == 0)
            def _():
                out[...] = jnp.zeros((128, 512), jnp.bfloat16)

            @pl.when(n > 0)
            def _():
                acc[...] = pair(at, 0, n)

                def more(p, c):
                    acc[...] += pair(at, p, n)
                    return c

                lax.fori_loop(1, (n + 1) // 2, more, 0)
                out[...] = acc[...].astype(jnp.bfloat16)

            return carry

        lax.fori_loop(0, 2, block, 0)


def rows(base, groups, lists, filled, tiles, sources, name):
    smem = pl.BlockSpec(memory_space=pltpu.SMEM)
    vmem = pl.BlockSpec(memory_space=pltpu.VMEM)
    return pl.pallas_call(
        functools.partial(rows_kernel, base, groups),
        out_shape=[jax.ShapeDtypeStruct((256, 512), jnp.bfloat16)] * groups,
        in_specs=[smem, smem, vmem, vmem],
        out_specs=[vmem] * groups,
        scratch_shapes=[pltpu.VMEM((128, 512), jnp.float32)],
        compiler_params=pltpu.CompilerParams(vmem_limit_bytes=16 * 1024 * 1024),
        cost_estimate=pl.CostEstimate(flops=groups * 400_000_000, bytes_accessed=groups * 1_000_000, transcendentals=0),
        name=name,
    )(lists, filled, tiles, sources)


def stage_kernel(sums, n_in, *refs):
    ins, outs = refs[:n_in], refs[n_in:]
    for out, terms in zip(outs, sums):
        total = None
        for at, start in terms:
            term = ins[at][pl.ds(start, out.shape[0]), :].astype(jnp.float32)
            total = term if total is None else total + term
        out[...] = total.astype(out.dtype)


def stage(name, *sums):
    arrays, plans, shapes = [], [], []
    for terms in sums:
        plan_of, rows_of = [], None
        for term in terms:
            value, start, count = term if isinstance(term, tuple) else (term, 0, term.shape[0])
            place = next((i for i, known in enumerate(arrays) if known is value), None)
            if place is None:
                place = len(arrays)
                arrays.append(value)
            plan_of.append((place, start))
            rows_of = count
        plans.append(tuple(plan_of))
        shapes.append(jax.ShapeDtypeStruct((rows_of, 512), jnp.bfloat16))
    vmem = pl.BlockSpec(memory_space=pltpu.VMEM)
    return pl.pallas_call(
        functools.partial(stage_kernel, tuple(plans), len(arrays)),
        out_shape=shapes,
        in_specs=[vmem] * len(arrays),
        out_specs=[vmem] * len(shapes),
        compiler_params=pltpu.CompilerParams(vmem_limit_bytes=16 * 1024 * 1024),
        name=name,
    )(*arrays)


def top(value):
    return (value, 0, 128)


def low(value):
    return (value, 128, 128)


def up(x, y, z, c):
    return (x, y, z + 1, c)


def down(x, y, z, c):
    return (x, y, z - 1, c)


def halves(value, bit):
    rows = value.shape[0] // 2
    kept = lax.dynamic_slice_in_dim(value, bit * rows, rows, 0)
    return kept, narrow(lax.dynamic_slice_in_dim(value, (1 - bit) * rows, rows, 0))


def joined(bit, value, got):
    return jnp.concatenate([jnp.where(bit == 0, value, got), jnp.where(bit == 0, got, value)])


def flipped(axis, step):
    def move(x, y, z, c):
        at = {"x": x, "y": y, "z": z, "c": c}
        at[axis] ^= step
        return at["x"], at["y"], at["z"], at["c"]

    return move


def local(grad_out, relu_mask, aggregated, weight, tile_values, tile_src, tile_dst, tile_count):
    row, rep = lax.axis_index("row"), lax.axis_index("rep")
    z, x_hi = row // 2, row % 2
    x_lo, y, core = rep // 8, (rep // 2) % 4, rep % 2
    place = jnp.stack([z, x_hi, core]).astype(jnp.int32)
    masked = jnp.where(relu_mask != 0, grad_out, jnp.zeros_like(grad_out))
    node_grad = lax.dot_general(
        masked, weight, (((1,), (1,)), ((), ())), preferred_element_type=jnp.float32
    ).astype(jnp.bfloat16)
    tiles = tile_values.reshape(SLOTS, 128, 128)
    lists, filled = plan(tile_src[0, 0], tile_dst[0, 0], tile_count[0, 0], place)
    aggregated, _ = lax.optimization_barrier((aggregated, node_grad))
    w = lax.dot_general(aggregated, masked, (((0,), (0,)), ((), ())), preferred_element_type=jnp.float32)

    even, odd = flood(node_grad, x_lo, y)
    kept, given = halves(w, core)
    w = add(kept, send(given, flipped("c", 1)))
    kept, given = halves(w, y % 2)
    w = add(kept, send(given, flipped("y", 1)))
    kept, given = halves(w, y // 2)
    even2, odd2 = send(even, flipped("c", 1)), send(odd, flipped("c", 1))
    even, odd, even2, odd2, given = stage("s0", [even], [odd], [even2], [odd2], [given])
    sources = jnp.concatenate([even, odd, even2, odd2]).reshape(8, 128, 512)
    w_got = send(given, flipped("y", 2))
    part = {}
    part.update(zip(FIRST, rows(0, len(FIRST), lists, filled, tiles, sources, "rows_first")))
    cross = flipped("x", 2)
    crossed = send(part[4, 1], cross)
    o_up, o_down = send(part[3, 1], up), send(part[5, 1], down)
    late = rows(2 * len(FIRST), len(SECOND), lists, filled, tiles, sources, "rows_second")
    part.update(zip(SECOND, late))

    a_up, b_down, w = stage(
        "s1", [top(part[4, 0]), top(crossed)], [low(part[4, 0]), low(crossed)], [narrow(add(kept, w_got))]
    )
    a_up, b_down, w_got = send(a_up, up), send(b_down, down), send(w, flipped("z", 1))
    o_up, o_down, w = stage("s2", [part[2, 1], o_up], [part[6, 1], o_down], [w, w_got])
    o_up, o_down, w_got = send(o_up, up), send(o_down, down), send(w, flipped("z", 2))
    a_up, b_up, a_down, b_down, w = stage(
        "s3",
        [top(part[3, 0]), a_up],
        [low(part[3, 0])],
        [top(part[5, 0])],
        [low(part[5, 0]), b_down],
        [w, w_got],
    )
    m_up, m_down = send(jnp.concatenate([a_up, b_up]), up), send(jnp.concatenate([a_down, b_down]), down)
    w_got = send(w, flipped("z", 4))
    o_up, o_down, w = stage("s4", [part[1, 1], o_up], [part[7, 1], o_down], [w, w_got])
    o_up, o_down, w_got = send(o_up, up), send(o_down, down), send(w, flipped("x", 1))
    m_up, m_down, w = stage("s5", [part[2, 0], m_up], [part[6, 0], m_down], [w, w_got])
    m_up, m_down, w_got = send(m_up, up), send(m_down, down), send(w, flipped("x", 2))
    crossing, w = stage("s6", [part[0, 1], o_up, o_down], [w, w_got])
    crossed, w_got = send(crossing, cross), send(w, flipped("y", 2))
    w = joined(y // 2, w, w_got)
    m_up, m_down, w = stage("s7", [part[1, 0], m_up], [part[7, 0], m_down], [w])
    m_up, m_down, w_got = send(m_up, up), send(m_down, down), send(w, flipped("y", 1))
    w = joined(y % 2, w, w_got)
    w = joined(core, w, send(w, flipped("c", 1)))
    (input_grad,) = stage("s8", [part[0, 0], m_up, m_down, crossed])
    return (input_grad, w.astype(jnp.float32))


def solution(mesh):
    in_specs = (
        P(("row", "rep"), None),
        P(("row", "rep"), None),
        P(("row", "rep"), None),
        P(),
        P("row", "rep", None, None, None, None),
        P("row", "rep", None, None),
        P("row", "rep", None, None),
        P("row", "rep", None),
    )
    out_specs = (P(("row", "rep"), None), P())
    return jax.shard_map(local, mesh=mesh, in_specs=in_specs, out_specs=out_specs, check_vma=False)
```

```python
import functools

import jax
import jax.numpy as jnp
from jax import lax
from jax.experimental import pallas as pl
from jax.experimental.pallas import tpu as pltpu
from jax.sharding import PartitionSpec as P

AXES = ("row", "rep")
X, Y, Z, C = 4, 4, 8, 2


def index_of(x, y, z, c):
    return (z * 2 + x // 2) * 16 + (x % 2) * 8 + y * 2 + c


def pairs(move):
    out = []
    for z in range(Z):
        for x in range(X):
            for y in range(Y):
                for c in range(C):
                    to = move(x, y, z, c)
                    if to is not None:
                        out.append((index_of(x, y, z, c), index_of(to[0] % X, to[1] % Y, to[2] % Z, to[3] % C)))
    return out


def send(value, move):
    return lax.ppermute(value, AXES, pairs(move))


def add(*terms):
    total = terms[0].astype(jnp.float32)
    for term in terms[1:]:
        total = total + term.astype(jnp.float32)
    return total


def narrow(value):
    return value.astype(jnp.bfloat16)


def across(x, y, z, c):
    return (x + 1, y, z, c) if x % 2 == 0 and y < 2 else None


def outward(x, y, z, c):
    return (x, 3 - y, z, c) if x % 2 == 0 and y < 2 else None


def swap(x, y, z, c):
    return (x, 1 - y, z, c) if x % 2 == 0 and y < 2 else None


def swap_rest(x, y, z, c):
    return (x, 5 - y, z, c) if x % 2 == 0 and y >= 2 else None


def across_all(x, y, z, c):
    return (x + 1, y, z, c) if x % 2 == 0 else None


def distant(x, y, z, c):
    return (x, y + 2, z, c) if x % 2 == 1 and y < 2 else None


FIRST = [(4, 1), (2, 1), (6, 1)]
SECOND = [(3, 1), (5, 1), (4, 0), (1, 1), (7, 1)]
THIRD = [(3, 0), (5, 0), (0, 1), (2, 0), (6, 0), (1, 0), (7, 0), (0, 0)]
SLOTS = 96


COUNT = 8
SPARE = 32


def plan_kernel(src_ref, dst_ref, count_ref, order_ref, given_ref, table_ref, passed_ref):
    row = lax.axis_index("row")
    z, xh, core = row // 2, lax.rem(row, 2), lax.rem(lax.axis_index("rep"), 2)
    for i in range(SPARE + 1):
        table_ref[i, COUNT] = 0
    for section in range(4):
        slot = jnp.where(core == section % 2, section // 2, 2 + section // 2)
        live = count_ref[section]

        def step(t, carry):
            d = dst_ref[section, t]
            rel = ((d >> 2) - z) & 7
            half = ((d >> 1) + xh) & 1
            at = jnp.where(t < live, order_ref[rel * 2 + half] * 2 + (d & 1), SPARE)
            n = table_ref[at, COUNT]
            table_ref[at, n & 7] = (section * 24 + t) * 8 + slot * 2 + src_ref[section, t]
            table_ref[at, COUNT] = n + 1
            return carry

        lax.fori_loop(0, 24, step, 0, unroll=True)
    passed_ref[...] = given_ref[...]


def plan(src, dst, count, given):
    order = [0] * 16
    for i, (rel, half) in enumerate(FIRST + SECOND + THIRD):
        order[rel * 2 + half] = i
    smem, vmem = pl.BlockSpec(memory_space=pltpu.SMEM), pl.BlockSpec(memory_space=pltpu.VMEM)
    return pl.pallas_call(
        plan_kernel,
        out_shape=[jax.ShapeDtypeStruct((SPARE + 1, 16), jnp.int32), jax.ShapeDtypeStruct(given.shape, given.dtype)],
        in_specs=[smem] * 4 + [vmem],
        out_specs=[smem, vmem],
        compiler_params=pltpu.CompilerParams(vmem_limit_bytes=10 * 1024 * 1024),
        name="plan",
    )(src, dst, count, jnp.array(order, jnp.int32), given)


def rows_kernel(base, sizes, table_ref, tiles_ref, sources_ref, *rest):
    outs, acc = rest[: len(sizes)], rest[len(sizes)]

    def pair(at, p, n):
        one = table_ref[at, 2 * p]
        paired = 2 * p + 1 < n
        two = jnp.where(paired, table_ref[at, 2 * p + 1], 0)
        second = tiles_ref[two // 8]
        left = jnp.concatenate([tiles_ref[one // 8], jnp.where(paired, second, jnp.zeros_like(second))], axis=0)
        right = jnp.concatenate([sources_ref[lax.rem(one, 8)], sources_ref[lax.rem(two, 8)]], axis=0)
        return lax.dot_general(left, right, (((0,), (0,)), ((), ())), preferred_element_type=jnp.float32)

    for g, size in enumerate(sizes):
        first = base + 2 * sum(sizes[:g])

        def block(j, carry):
            at = first + j
            n = table_ref[at, COUNT]
            out = outs[g].at[pl.ds(pl.multiple_of(j * 128, 128), 128), :]

            @pl.when(n == 0)
            def _():
                out[...] = jnp.zeros((128, 512), jnp.bfloat16)

            @pl.when(n > 0)
            def _():
                acc[...] = pair(at, 0, n)

                def more(p, c):
                    acc[...] += pair(at, p, n)
                    return c

                lax.fori_loop(1, (n + 1) // 2, more, 0)
                out[...] = acc[...].astype(jnp.bfloat16)

            return carry

        lax.fori_loop(0, 2 * size, block, 0)


def rows(base, sizes, table, tiles, sources, name):
    smem = pl.BlockSpec(memory_space=pltpu.SMEM)
    vmem = pl.BlockSpec(memory_space=pltpu.VMEM)
    return pl.pallas_call(
        functools.partial(rows_kernel, base, tuple(sizes)),
        out_shape=[jax.ShapeDtypeStruct((256 * size, 512), jnp.bfloat16) for size in sizes],
        in_specs=[smem, vmem, vmem],
        out_specs=[vmem] * len(sizes),
        scratch_shapes=[pltpu.VMEM((128, 512), jnp.float32)],
        compiler_params=pltpu.CompilerParams(vmem_limit_bytes=10 * 1024 * 1024),
        cost_estimate=pl.CostEstimate(flops=sum(sizes) * 400_000_000, bytes_accessed=1_000_000, transcendentals=0),
        name=name,
    )(table, tiles, sources)


def stage_kernel(plans, n_in, n_anchors, *refs):
    ins, outs = refs[:n_in], refs[n_in + n_anchors :]
    for out, segments in zip(outs, plans):
        at = 0
        for count, terms in segments:
            values = [ins[i][pl.ds(start, count), :].astype(jnp.float32) for i, start in terms]
            while len(values) > 1:
                values = [sum(values[i : i + 2]) for i in range(0, len(values), 2)]
            out[pl.ds(at, count), :] = values[0].astype(out.dtype)
            at += count


def stage(name, *outputs, anchors=()):
    arrays, plans, shapes = [], [], []
    for segments in outputs:
        planned = []
        for count, *terms in segments:
            numbered = []
            for term in terms:
                value, start = term if isinstance(term, tuple) else (term, 0)
                place = next((i for i, known in enumerate(arrays) if known is value), None)
                if place is None:
                    place = len(arrays)
                    arrays.append(value)
                numbered.append((place, start))
            planned.append((count, tuple(numbered)))
        plans.append(tuple(planned))
        shapes.append(jax.ShapeDtypeStruct((sum(count for count, _ in planned), 512), jnp.bfloat16))
    vmem, anywhere = pl.BlockSpec(memory_space=pltpu.VMEM), pl.BlockSpec(memory_space=pl.ANY)
    return pl.pallas_call(
        functools.partial(stage_kernel, tuple(plans), len(arrays), len(anchors)),
        out_shape=shapes,
        in_specs=[vmem] * len(arrays) + [anywhere if anchor.dtype == jnp.int32 else vmem for anchor in anchors],
        out_specs=[vmem] * len(shapes),
        compiler_params=pltpu.CompilerParams(vmem_limit_bytes=6 * 1024 * 1024),
        cost_estimate=pl.CostEstimate(flops=1000, bytes_accessed=1000, transcendentals=0),
        name=name,
    )(*arrays, *anchors)


def up(x, y, z, c):
    return (x, y, z + 1, c)


def down(x, y, z, c):
    return (x, y, z - 1, c)


def halves(value, bit):
    rows = value.shape[0] // 2
    kept = lax.dynamic_slice_in_dim(value, bit * rows, rows, 0)
    return kept, narrow(lax.dynamic_slice_in_dim(value, (1 - bit) * rows, rows, 0))


def joined(bit, value, got):
    return jnp.concatenate([jnp.where(bit == 0, value, got), jnp.where(bit == 0, got, value)])


def later(name, anchor, *terms):
    return stage(name, [(terms[0].shape[0], *terms)], anchors=(anchor,))[0]


def flipped(axis, step):
    def move(x, y, z, c):
        at = {"x": x, "y": y, "z": z, "c": c}
        at[axis] ^= step
        return at["x"], at["y"], at["z"], at["c"]

    return move


def local(grad_out, relu_mask, aggregated, weight, tile_values, tile_src, tile_dst, tile_count):
    rep = lax.axis_index("rep")
    x_lo, y, core = rep // 8, (rep // 2) % 4, rep % 2
    other, cross = flipped("c", 1), flipped("x", 2)
    tiles = tile_values.reshape(SLOTS, 128, 128)

    masked = jnp.where(relu_mask != 0, grad_out, jnp.zeros_like(grad_out))
    node_grad = lax.dot_general(
        masked, weight, (((1,), (1,)), ((), ())), preferred_element_type=jnp.float32
    ).astype(jnp.bfloat16)
    w = lax.dot_general(aggregated, masked, (((0,), (0,)), ((), ())), preferred_element_type=jnp.float32)
    kept, given = halves(w, core)
    by_x, by_y, swapped = send(node_grad, across), send(node_grad, outward), send(node_grad, swap)
    w = add(kept, send(given, other))
    kept, given = halves(w, y % 2)
    table, given = plan(tile_src[0, 0], tile_dst[0, 0], tile_count[0, 0], given)
    onward = jnp.where(y < 2, swapped, by_y)
    by_x2, by_far, by_swap = send(onward, across_all), send(by_x, distant), send(by_y, swap_rest)
    w = add(kept, send(given, flipped("y", 1)))
    first = jnp.where(x_lo == 0, jnp.where(y < 2, node_grad, by_y), jnp.where(y < 2, by_x, by_x2))
    second = jnp.where(x_lo == 0, jnp.where(y < 2, swapped, by_swap), jnp.where(y < 2, by_x2, by_far))
    flip = jnp.logical_or(y == 1, y == 2)
    even, odd = jnp.where(flip, second, first), jnp.where(flip, first, second)

    even2, odd2 = send(even, other), send(odd, other)
    w = narrow(w)
    w_got = send(w, flipped("z", 1))
    sources, w = stage(
        "s0", [(256, even), (256, odd), (256, even2), (256, odd2)], [(128, w, w_got)]
    )
    sources = sources.reshape(8, 128, 512)

    t4, t2, t6 = rows(0, [1, 1, 1], table, tiles, sources, "rows_first")
    x4, up_got, down_got = send(t4, cross), send(t2, up), send(t6, down)
    kept, given = halves(w, y // 2)
    w_got = send(given, flipped("y", 2))
    t35, m4, t1, t7 = rows(6, [2, 1, 1, 1], table, tiles, sources, "rows_second")
    to_up, to_down, t35, w = stage(
        "s1",
        [(256, t1, up_got), (128, m4, x4)],
        [(256, t7, down_got), (128, (m4, 128), (x4, 128))],
        [(512, t35)],
        [(64, kept, w_got)],
    )

    up_t, down_t, x35 = send(to_up, up), send(to_down, down), send(t35, cross)
    w = narrow(add(w, send(w, flipped("z", 2))))
    w_got = send(w, flipped("z", 4))
    m3, m5, t0, m2, m6, m1, m7, m0 = rows(16, [1] * 8, table, tiles, sources, "rows_third")
    to_up, to_down, w = stage(
        "s2",
        [(128, m3, x35, (up_t, 256)), (128, (m3, 128), (x35, 128))],
        [(128, m5, (x35, 256)), (128, (m5, 128), (x35, 384), (down_t, 256))],
        [(64, w, w_got)],
    )

    up_got, down_got = send(to_up, up), send(to_down, down)
    w_got = [send(w, flipped("x", step)) for step in (1, 2, 3)]
    to_up, to_down, w = stage("s3", [(256, m2, up_got)], [(256, m6, down_got)], [(64, w, *w_got)])

    up_got, down_got = send(to_up, up), send(to_down, down)
    w_got = [send(w, flipped("y", step)) for step in (1, 2, 3)]
    to_up, to_down, crossing = stage(
        "s4", [(256, m1, up_got)], [(256, m7, down_got)], [(256, t0, up_t, down_t)]
    )
    w = stage("v5", *[[(64, piece)] for piece in (w, *w_got)], anchors=(to_up,))
    w = joined(y % 2, joined(y // 2, w[0], w[2]), joined(y // 2, w[1], w[3]))

    up_got, down_got, crossed = send(to_up, up), send(to_down, down), send(crossing, cross)
    w_got = send(w, other)
    (input_grad,) = stage("s5", [(256, m0, up_got, down_got, crossed)])
    return (input_grad, joined(core, w, w_got).astype(jnp.float32))


def solution(mesh):
    in_specs = (
        P(("row", "rep"), None),
        P(("row", "rep"), None),
        P(("row", "rep"), None),
        P(),
        P("row", "rep", None, None, None, None),
        P("row", "rep", None, None),
        P("row", "rep", None, None),
        P("row", "rep", None),
    )
    out_specs = (P(("row", "rep"), None), P())
    return jax.shard_map(local, mesh=mesh, in_specs=in_specs, out_specs=out_specs, check_vma=False)
```

```python
import functools

import jax
import jax.numpy as jnp
from jax import lax
from jax.experimental import pallas as pl
from jax.experimental.pallas import tpu as pltpu
from jax.sharding import PartitionSpec as P

AXES = ("row", "rep")
X, Y, Z, C = 4, 4, 8, 2


def index_of(x, y, z, c):
    return (z * 2 + x // 2) * 16 + (x % 2) * 8 + y * 2 + c


def pairs(move):
    out = []
    for z in range(Z):
        for x in range(X):
            for y in range(Y):
                for c in range(C):
                    to = move(x, y, z, c)
                    if to is not None:
                        out.append((index_of(x, y, z, c), index_of(to[0] % X, to[1] % Y, to[2] % Z, to[3] % C)))
    return out


def send(value, move):
    return lax.ppermute(value, AXES, pairs(move))


def add(*terms):
    total = terms[0].astype(jnp.float32)
    for term in terms[1:]:
        total = total + term.astype(jnp.float32)
    return total


def narrow(value):
    return value.astype(jnp.bfloat16)


def across(x, y, z, c):
    return (x + 1, y, z, c) if x % 2 == 0 and y < 2 else None


def outward(x, y, z, c):
    return (x, 3 - y, z, c) if x % 2 == 0 and y < 2 else None


def swap(x, y, z, c):
    return (x, 1 - y, z, c) if x % 2 == 0 and y < 2 else None


def swap_rest(x, y, z, c):
    return (x, 5 - y, z, c) if x % 2 == 0 and y >= 2 else None


def across_all(x, y, z, c):
    return (x + 1, y, z, c) if x % 2 == 0 else None


def distant(x, y, z, c):
    return (x, y + 2, z, c) if x % 2 == 1 and y < 2 else None


FIRST = [(4, 1), (2, 1), (6, 1)]
SECOND = [(3, 1), (5, 1), (4, 0), (1, 1), (7, 1)]
THIRD = [(3, 0), (5, 0), (0, 1), (2, 0), (6, 0), (1, 0), (7, 0), (0, 0)]
SLOTS = 96


COUNT = 8
SPARE = 32


def plan_kernel(src_ref, dst_ref, count_ref, order_ref, given_ref, table_ref, passed_ref):
    row = lax.axis_index("row")
    z, xh, core = row // 2, lax.rem(row, 2), lax.rem(lax.axis_index("rep"), 2)
    for i in range(SPARE + 1):
        table_ref[i, COUNT] = 0
    for section in range(4):
        slot = jnp.where(core == section % 2, section // 2, 2 + section // 2)
        live = count_ref[section]

        def step(t, carry):
            d = dst_ref[section, t]
            rel = ((d >> 2) - z) & 7
            half = ((d >> 1) + xh) & 1
            at = jnp.where(t < live, order_ref[rel * 2 + half] * 2 + (d & 1), SPARE)
            n = table_ref[at, COUNT]
            table_ref[at, n & 7] = (section * 24 + t) * 8 + slot * 2 + src_ref[section, t]
            table_ref[at, COUNT] = n + 1
            return carry

        lax.fori_loop(0, 24, step, 0, unroll=True)
    passed_ref[...] = given_ref[...]


def plan(src, dst, count, given):
    order = [0] * 16
    for i, (rel, half) in enumerate(FIRST + SECOND + THIRD):
        order[rel * 2 + half] = i
    smem, vmem = pl.BlockSpec(memory_space=pltpu.SMEM), pl.BlockSpec(memory_space=pltpu.VMEM)
    return pl.pallas_call(
        plan_kernel,
        out_shape=[jax.ShapeDtypeStruct((SPARE + 1, 16), jnp.int32), jax.ShapeDtypeStruct(given.shape, given.dtype)],
        in_specs=[smem] * 4 + [vmem],
        out_specs=[smem, vmem],
        compiler_params=pltpu.CompilerParams(vmem_limit_bytes=10 * 1024 * 1024),
        name="plan",
    )(src, dst, count, jnp.array(order, jnp.int32), given)


def rows_kernel(base, sizes, table_ref, tiles_ref, sources_ref, *rest):
    outs, acc = rest[: len(sizes)], rest[len(sizes)]

    def masked(at, slot, n):
        live = slot < n
        code = jnp.where(live, table_ref[at, slot], 0)
        tile = tiles_ref[code >> 3]
        return jnp.where(live, tile, jnp.zeros_like(tile)), sources_ref[code & 7]

    def pair(at, p, n):
        (left, right), (left2, right2) = masked(at, 2 * p, n), masked(at, 2 * p + 1, n)
        return lax.dot_general(
            jnp.concatenate([left, left2], axis=0),
            jnp.concatenate([right, right2], axis=0),
            (((0,), (0,)), ((), ())),
            preferred_element_type=jnp.float32,
        )

    for g, size in enumerate(sizes):
        first = base + 2 * sum(sizes[:g])

        def blocks(j, carry):
            at = first + 2 * j
            n, n2 = table_ref[at, COUNT], table_ref[at + 1, COUNT]
            acc[0] = pair(at, 0, n)
            acc[1] = pair(at + 1, 0, n2)

            def more(p, c):
                acc[0] += pair(at, p, n)
                acc[1] += pair(at + 1, p, n2)
                return c

            lax.fori_loop(1, (jnp.maximum(n, n2) + 1) // 2, more, 0)
            start = pl.multiple_of(j * 256, 256)
            outs[g][pl.ds(start, 128), :] = acc[0].astype(jnp.bfloat16)
            outs[g][pl.ds(start + 128, 128), :] = acc[1].astype(jnp.bfloat16)
            return carry

        lax.fori_loop(0, size, blocks, 0)


def rows(base, sizes, table, tiles, sources, name):
    smem = pl.BlockSpec(memory_space=pltpu.SMEM)
    vmem = pl.BlockSpec(memory_space=pltpu.VMEM)
    return pl.pallas_call(
        functools.partial(rows_kernel, base, tuple(sizes)),
        out_shape=[jax.ShapeDtypeStruct((256 * size, 512), jnp.bfloat16) for size in sizes],
        in_specs=[smem, vmem, vmem],
        out_specs=[vmem] * len(sizes),
        scratch_shapes=[pltpu.VMEM((2, 128, 512), jnp.float32)],
        compiler_params=pltpu.CompilerParams(vmem_limit_bytes=10 * 1024 * 1024),
        cost_estimate=pl.CostEstimate(flops=sum(sizes) * 400_000_000, bytes_accessed=1_000_000, transcendentals=0),
        name=name,
    )(table, tiles, sources)


def stage_kernel(plans, n_in, n_anchors, *refs):
    ins, outs = refs[:n_in], refs[n_in + n_anchors :]
    for out, segments in zip(outs, plans):
        at = 0
        for count, terms in segments:
            values = [ins[i][pl.ds(start, count), :].astype(jnp.float32) for i, start in terms]
            while len(values) > 1:
                values = [sum(values[i : i + 2]) for i in range(0, len(values), 2)]
            out[pl.ds(at, count), :] = values[0].astype(out.dtype)
            at += count


def stage(name, *outputs, anchors=()):
    arrays, plans, shapes = [], [], []
    for segments in outputs:
        planned = []
        for count, *terms in segments:
            numbered = []
            for term in terms:
                value, start = term if isinstance(term, tuple) else (term, 0)
                place = next((i for i, known in enumerate(arrays) if known is value), None)
                if place is None:
                    place = len(arrays)
                    arrays.append(value)
                numbered.append((place, start))
            planned.append((count, tuple(numbered)))
        plans.append(tuple(planned))
        shapes.append(jax.ShapeDtypeStruct((sum(count for count, _ in planned), 512), jnp.bfloat16))
    vmem, anywhere = pl.BlockSpec(memory_space=pltpu.VMEM), pl.BlockSpec(memory_space=pl.ANY)
    return pl.pallas_call(
        functools.partial(stage_kernel, tuple(plans), len(arrays), len(anchors)),
        out_shape=shapes,
        in_specs=[vmem] * len(arrays) + [anywhere if anchor.dtype == jnp.int32 else vmem for anchor in anchors],
        out_specs=[vmem] * len(shapes),
        compiler_params=pltpu.CompilerParams(vmem_limit_bytes=6 * 1024 * 1024),
        cost_estimate=pl.CostEstimate(flops=1000, bytes_accessed=1000, transcendentals=0),
        name=name,
    )(*arrays, *anchors)


def up(x, y, z, c):
    return (x, y, z + 1, c)


def down(x, y, z, c):
    return (x, y, z - 1, c)


def halves(value, bit):
    rows = value.shape[0] // 2
    kept = lax.dynamic_slice_in_dim(value, bit * rows, rows, 0)
    return kept, narrow(lax.dynamic_slice_in_dim(value, (1 - bit) * rows, rows, 0))


def joined(bit, value, got):
    return jnp.concatenate([jnp.where(bit == 0, value, got), jnp.where(bit == 0, got, value)])


def later(name, anchor, *terms):
    return stage(name, [(terms[0].shape[0], *terms)], anchors=(anchor,))[0]


def flipped(axis, step):
    def move(x, y, z, c):
        at = {"x": x, "y": y, "z": z, "c": c}
        at[axis] ^= step
        return at["x"], at["y"], at["z"], at["c"]

    return move


def local(grad_out, relu_mask, aggregated, weight, tile_values, tile_src, tile_dst, tile_count):
    rep = lax.axis_index("rep")
    x_lo, y, core = rep // 8, (rep // 2) % 4, rep % 2
    other, cross = flipped("c", 1), flipped("x", 2)
    tiles = tile_values.reshape(SLOTS, 128, 128)

    masked = jnp.where(relu_mask != 0, grad_out, jnp.zeros_like(grad_out))
    node_grad = lax.dot_general(
        masked, weight, (((1,), (1,)), ((), ())), preferred_element_type=jnp.float32
    ).astype(jnp.bfloat16)
    w = lax.dot_general(aggregated, masked, (((0,), (0,)), ((), ())), preferred_element_type=jnp.float32)
    kept, given = halves(w, core)
    table, given = plan(tile_src[0, 0], tile_dst[0, 0], tile_count[0, 0], given)
    by_x, by_y, swapped = send(node_grad, across), send(node_grad, outward), send(node_grad, swap)
    w = add(kept, send(given, other))
    kept, given = halves(w, y % 2)
    onward = jnp.where(y < 2, swapped, by_y)
    by_x2, by_far, by_swap = send(onward, across_all), send(by_x, distant), send(by_y, swap_rest)
    w = add(kept, send(given, flipped("y", 1)))
    first = jnp.where(x_lo == 0, jnp.where(y < 2, node_grad, by_y), jnp.where(y < 2, by_x, by_x2))
    second = jnp.where(x_lo == 0, jnp.where(y < 2, swapped, by_swap), jnp.where(y < 2, by_x2, by_far))
    flip = jnp.logical_or(y == 1, y == 2)
    even, odd = jnp.where(flip, second, first), jnp.where(flip, first, second)

    even2, odd2 = send(even, other), send(odd, other)
    sources, w = stage("s0", [(256, even), (256, odd), (256, even2), (256, odd2)], [(128, narrow(w))])
    sources = sources.reshape(8, 128, 512)

    w_got = send(w, flipped("z", 1))
    t4, t2, t6 = rows(0, [1, 1, 1], table, tiles, sources, "rows_first")
    x4, up_got, down_got = send(t4, cross), send(t2, up), send(t6, down)
    kept, given = halves(later("v1", t4, w, w_got), y // 2)
    w_got = send(given, flipped("y", 2))
    t35, m4, t1, t7 = rows(6, [2, 1, 1, 1], table, tiles, sources, "rows_second")
    to_up, to_down, t35, w = stage(
        "s1",
        [(256, t1, up_got), (128, m4, x4)],
        [(256, t7, down_got), (128, (m4, 128), (x4, 128))],
        [(512, t35)],
        [(64, kept, w_got)],
    )

    up_t, down_t, x35 = send(to_up, up), send(to_down, down), send(t35, cross)
    w = narrow(add(w, send(w, flipped("z", 2))))
    w_got = send(w, flipped("z", 4))
    m3, m5, t0, m2, m6, m1, m7, m0 = rows(16, [1] * 8, table, tiles, sources, "rows_third")
    to_up, to_down, w = stage(
        "s2",
        [(128, m3, x35, (up_t, 256)), (128, (m3, 128), (x35, 128))],
        [(128, m5, (x35, 256)), (128, (m5, 128), (x35, 384), (down_t, 256))],
        [(64, w, w_got)],
    )

    up_got, down_got = send(to_up, up), send(to_down, down)
    w_got = [send(w, flipped("x", step)) for step in (1, 2, 3)]
    to_up, to_down, w = stage("s3", [(256, m2, up_got)], [(256, m6, down_got)], [(64, w, *w_got)])

    up_got, down_got = send(to_up, up), send(to_down, down)
    w_got = [send(w, flipped("y", step)) for step in (1, 2, 3)]
    to_up, to_down, crossing = stage(
        "s4", [(256, m1, up_got)], [(256, m7, down_got)], [(256, t0, up_t, down_t)]
    )
    w = stage("v5", *[[(64, piece)] for piece in (w, *w_got)], anchors=(to_up,))
    w = joined(y % 2, joined(y // 2, w[0], w[2]), joined(y // 2, w[1], w[3]))

    up_got, down_got, crossed = send(to_up, up), send(to_down, down), send(crossing, cross)
    w_got = send(w, other)
    (input_grad,) = stage("s5", [(256, m0, up_got, down_got, crossed)])
    return (input_grad, joined(core, w, w_got).astype(jnp.float32))


def solution(mesh):
    in_specs = (
        P(("row", "rep"), None),
        P(("row", "rep"), None),
        P(("row", "rep"), None),
        P(),
        P("row", "rep", None, None, None, None),
        P("row", "rep", None, None),
        P("row", "rep", None, None),
        P("row", "rep", None),
    )
    out_specs = (P(("row", "rep"), None), P())
    return jax.shard_map(local, mesh=mesh, in_specs=in_specs, out_specs=out_specs, check_vma=False)
```

```python
import functools

import jax
import jax.numpy as jnp
from jax import lax
from jax.experimental import pallas as pl
from jax.experimental.pallas import tpu as pltpu
from jax.sharding import PartitionSpec as P

AXES = ("row", "rep")
X, Y, Z, C = 4, 4, 8, 2


def index_of(x, y, z, c):
    return (z * 2 + x // 2) * 16 + (x % 2) * 8 + y * 2 + c


def pairs(move):
    out = []
    for z in range(Z):
        for x in range(X):
            for y in range(Y):
                for c in range(C):
                    to = move(x, y, z, c)
                    if to is not None:
                        out.append((index_of(x, y, z, c), index_of(to[0] % X, to[1] % Y, to[2] % Z, to[3] % C)))
    return out


def send(value, move):
    return lax.ppermute(value, AXES, pairs(move))


def add(*terms):
    total = terms[0].astype(jnp.float32)
    for term in terms[1:]:
        total = total + term.astype(jnp.float32)
    return total


def narrow(value):
    return value.astype(jnp.bfloat16)


def across(x, y, z, c):
    return (x + 1, y, z, c) if x % 2 == 0 and y < 2 else None


def outward(x, y, z, c):
    return (x, 3 - y, z, c) if x % 2 == 0 and y < 2 else None


def swap(x, y, z, c):
    return (x, 1 - y, z, c) if x % 2 == 0 and y < 2 else None


def swap_rest(x, y, z, c):
    return (x, 5 - y, z, c) if x % 2 == 0 and y >= 2 else None


def across_all(x, y, z, c):
    return (x + 1, y, z, c) if x % 2 == 0 else None


def distant(x, y, z, c):
    return (x, y + 2, z, c) if x % 2 == 1 and y < 2 else None


FIRST = [(4, 1), (2, 1), (6, 1)]
SECOND = [(3, 1), (5, 1), (4, 0), (1, 1), (7, 1)]
THIRD = [(3, 0), (5, 0), (0, 1), (2, 0), (6, 0), (1, 0), (7, 0), (0, 0)]
SLOTS = 96


COUNT = 8
SPARE = 32


def plan_kernel(src_ref, dst_ref, count_ref, order_ref, given_ref, table_ref, passed_ref):
    row = lax.axis_index("row")
    z, xh, core = row // 2, lax.rem(row, 2), lax.rem(lax.axis_index("rep"), 2)
    for i in range(SPARE + 1):
        table_ref[i, COUNT] = 0
    for section in range(4):
        slot = jnp.where(core == section % 2, section // 2, 2 + section // 2)
        live = count_ref[section]

        def step(t, carry):
            d = dst_ref[section, t]
            rel = ((d >> 2) - z) & 7
            half = ((d >> 1) + xh) & 1
            at = jnp.where(t < live, order_ref[rel * 2 + half] * 2 + (d & 1), SPARE)
            n = table_ref[at, COUNT]
            table_ref[at, n & 7] = (section * 24 + t) * 8 + slot * 2 + src_ref[section, t]
            table_ref[at, COUNT] = n + 1
            return carry

        lax.fori_loop(0, 24, step, 0, unroll=True)
    passed_ref[...] = given_ref[...]


def plan(src, dst, count, given):
    order = [0] * 16
    for i, (rel, half) in enumerate(FIRST + SECOND + THIRD):
        order[rel * 2 + half] = i
    smem, vmem = pl.BlockSpec(memory_space=pltpu.SMEM), pl.BlockSpec(memory_space=pltpu.VMEM)
    return pl.pallas_call(
        plan_kernel,
        out_shape=[jax.ShapeDtypeStruct((SPARE + 1, 16), jnp.int32), jax.ShapeDtypeStruct(given.shape, given.dtype)],
        in_specs=[smem] * 4 + [vmem],
        out_specs=[smem, vmem],
        compiler_params=pltpu.CompilerParams(vmem_limit_bytes=10 * 1024 * 1024),
        name="plan",
    )(src, dst, count, jnp.array(order, jnp.int32), given)


def rows_kernel(base, sizes, table_ref, tiles_ref, sources_ref, *rest):
    outs, acc = rest[: len(sizes)], rest[len(sizes)]

    def masked(at, slot, n):
        live = slot < n
        code = jnp.where(live, table_ref[at, slot], 0)
        tile = tiles_ref[code >> 3]
        return jnp.where(live, tile, jnp.zeros_like(tile)), sources_ref[code & 7]

    def pair(at, p, n):
        (left, right), (left2, right2) = masked(at, 2 * p, n), masked(at, 2 * p + 1, n)
        return lax.dot_general(
            jnp.concatenate([left, left2], axis=0),
            jnp.concatenate([right, right2], axis=0),
            (((0,), (0,)), ((), ())),
            preferred_element_type=jnp.float32,
        )

    for g, size in enumerate(sizes):
        first = base + 2 * sum(sizes[:g])

        def blocks(j, carry):
            at = first + 2 * j
            n, n2 = table_ref[at, COUNT], table_ref[at + 1, COUNT]
            acc[0] = pair(at, 0, n)
            acc[1] = pair(at + 1, 0, n2)

            def more(p, c):
                acc[0] += pair(at, p, n)
                acc[1] += pair(at + 1, p, n2)
                return c

            lax.fori_loop(1, (jnp.maximum(n, n2) + 1) // 2, more, 0)
            start = pl.multiple_of(j * 256, 256)
            outs[g][pl.ds(start, 128), :] = acc[0].astype(jnp.bfloat16)
            outs[g][pl.ds(start + 128, 128), :] = acc[1].astype(jnp.bfloat16)
            return carry

        lax.fori_loop(0, size, blocks, 0)


def rows(base, sizes, table, tiles, sources, name):
    smem = pl.BlockSpec(memory_space=pltpu.SMEM)
    vmem = pl.BlockSpec(memory_space=pltpu.VMEM)
    return pl.pallas_call(
        functools.partial(rows_kernel, base, tuple(sizes)),
        out_shape=[jax.ShapeDtypeStruct((256 * size, 512), jnp.bfloat16) for size in sizes],
        in_specs=[smem, vmem, vmem],
        out_specs=[vmem] * len(sizes),
        scratch_shapes=[pltpu.VMEM((2, 128, 512), jnp.float32)],
        compiler_params=pltpu.CompilerParams(vmem_limit_bytes=10 * 1024 * 1024),
        cost_estimate=pl.CostEstimate(flops=sum(sizes) * 400_000_000, bytes_accessed=1_000_000, transcendentals=0),
        name=name,
    )(table, tiles, sources)


def stage_kernel(plans, n_in, n_anchors, *refs):
    ins, outs = refs[:n_in], refs[n_in + n_anchors :]
    for out, segments in zip(outs, plans):
        at = 0
        for count, terms in segments:
            values = [ins[i][pl.ds(start, count), :].astype(jnp.float32) for i, start in terms]
            while len(values) > 1:
                values = [sum(values[i : i + 2]) for i in range(0, len(values), 2)]
            out[pl.ds(at, count), :] = values[0].astype(out.dtype)
            at += count


def collect_kernel(plans, n_in, pieces, *refs):
    stage_kernel(plans, n_in, pieces, *refs[:-1])
    y = lax.rem(lax.axis_index("rep") // 2, 4)
    for step in range(pieces):
        owner = y ^ step
        start = pl.multiple_of((owner & 1) * 128 + (owner >> 1) * 64, 64)
        refs[-1][pl.ds(start, 64), :] = refs[n_in + step][...]


def stage(name, *outputs, anchors=(), collect=False):
    arrays, plans, shapes = [], [], []
    for segments in outputs:
        planned = []
        for count, *terms in segments:
            numbered = []
            for term in terms:
                value, start = term if isinstance(term, tuple) else (term, 0)
                place = next((i for i, known in enumerate(arrays) if known is value), None)
                if place is None:
                    place = len(arrays)
                    arrays.append(value)
                numbered.append((place, start))
            planned.append((count, tuple(numbered)))
        plans.append(tuple(planned))
        shapes.append(jax.ShapeDtypeStruct((sum(count for count, _ in planned), 512), jnp.bfloat16))
    if collect:
        shapes.append(jax.ShapeDtypeStruct((256, 512), jnp.bfloat16))
    vmem, anywhere = pl.BlockSpec(memory_space=pltpu.VMEM), pl.BlockSpec(memory_space=pl.ANY)
    return pl.pallas_call(
        functools.partial(collect_kernel if collect else stage_kernel, tuple(plans), len(arrays), len(anchors)),
        out_shape=shapes,
        in_specs=[vmem] * len(arrays) + [anywhere if anchor.dtype == jnp.int32 else vmem for anchor in anchors],
        out_specs=[vmem] * len(shapes),
        compiler_params=pltpu.CompilerParams(vmem_limit_bytes=6 * 1024 * 1024),
        cost_estimate=pl.CostEstimate(flops=1000, bytes_accessed=1000, transcendentals=0),
        name=name,
    )(*arrays, *anchors)


def up(x, y, z, c):
    return (x, y, z + 1, c)


def down(x, y, z, c):
    return (x, y, z - 1, c)


def halves(value, bit):
    rows = value.shape[0] // 2
    kept = lax.dynamic_slice_in_dim(value, bit * rows, rows, 0)
    return kept, narrow(lax.dynamic_slice_in_dim(value, (1 - bit) * rows, rows, 0))


def joined(bit, value, got):
    return jnp.concatenate([jnp.where(bit == 0, value, got), jnp.where(bit == 0, got, value)])


def later(name, anchor, *terms):
    return stage(name, [(terms[0].shape[0], *terms)], anchors=(anchor,))[0]


def flipped(axis, step):
    def move(x, y, z, c):
        at = {"x": x, "y": y, "z": z, "c": c}
        at[axis] ^= step
        return at["x"], at["y"], at["z"], at["c"]

    return move


def local(grad_out, relu_mask, aggregated, weight, tile_values, tile_src, tile_dst, tile_count):
    rep = lax.axis_index("rep")
    x_lo, y, core = rep // 8, (rep // 2) % 4, rep % 2
    other, cross = flipped("c", 1), flipped("x", 2)
    tiles = tile_values.reshape(SLOTS, 128, 128)

    masked = jnp.where(relu_mask != 0, grad_out, jnp.zeros_like(grad_out))
    node_grad = lax.dot_general(
        masked, weight, (((1,), (1,)), ((), ())), preferred_element_type=jnp.float32
    ).astype(jnp.bfloat16)
    w = lax.dot_general(aggregated, masked, (((0,), (0,)), ((), ())), preferred_element_type=jnp.float32)
    kept, given = halves(w, core)
    table, given = plan(tile_src[0, 0], tile_dst[0, 0], tile_count[0, 0], given)
    by_x, by_y, swapped = send(node_grad, across), send(node_grad, outward), send(node_grad, swap)
    w = add(kept, send(given, other))
    kept, given = halves(w, y % 2)
    onward = jnp.where(y < 2, swapped, by_y)
    by_x2, by_far, by_swap = send(onward, across_all), send(by_x, distant), send(by_y, swap_rest)
    w = add(kept, send(given, flipped("y", 1)))
    first = jnp.where(x_lo == 0, jnp.where(y < 2, node_grad, by_y), jnp.where(y < 2, by_x, by_x2))
    second = jnp.where(x_lo == 0, jnp.where(y < 2, swapped, by_swap), jnp.where(y < 2, by_x2, by_far))
    flip = jnp.logical_or(y == 1, y == 2)
    even, odd = jnp.where(flip, second, first), jnp.where(flip, first, second)

    even2, odd2 = send(even, other), send(odd, other)
    sources, w = stage("s0", [(256, even), (256, odd), (256, even2), (256, odd2)], [(128, narrow(w))])
    sources = sources.reshape(8, 128, 512)

    w_got = send(w, flipped("z", 1))
    t4, t2, t6 = rows(0, [1, 1, 1], table, tiles, sources, "rows_first")
    x4, up_got, down_got = send(t4, cross), send(t2, up), send(t6, down)
    kept, given = halves(later("v1", t4, w, w_got), y // 2)
    w_got = send(given, flipped("y", 2))
    t35, m4, t1, t7 = rows(6, [2, 1, 1, 1], table, tiles, sources, "rows_second")
    to_up, to_down, t35, w = stage(
        "s1",
        [(256, t1, up_got), (128, m4, x4)],
        [(256, t7, down_got), (128, (m4, 128), (x4, 128))],
        [(512, t35)],
        [(64, kept, w_got)],
    )

    up_t, down_t, x35 = send(to_up, up), send(to_down, down), send(t35, cross)
    w = narrow(add(w, send(w, flipped("z", 2))))
    w_got = send(w, flipped("z", 4))
    m3, m5, t0, m2, m6, m1, m7, m0 = rows(16, [1] * 8, table, tiles, sources, "rows_third")
    to_up, to_down, w = stage(
        "s2",
        [(128, m3, x35, (up_t, 256)), (128, (m3, 128), (x35, 128))],
        [(128, m5, (x35, 256)), (128, (m5, 128), (x35, 384), (down_t, 256))],
        [(64, w, w_got)],
    )

    up_got, down_got = send(to_up, up), send(to_down, down)
    w_got = [send(w, flipped("x", step)) for step in (1, 2, 3)]
    to_up, to_down, w = stage("s3", [(256, m2, up_got)], [(256, m6, down_got)], [(64, w, *w_got)])

    up_got, down_got = send(to_up, up), send(to_down, down)
    w_got = [send(w, flipped("y", step)) for step in (1, 2, 3)]
    to_up, to_down, crossing, w = stage(
        "s4",
        [(256, m1, up_got)],
        [(256, m7, down_got)],
        [(256, t0, up_t, down_t)],
        anchors=(w, *w_got),
        collect=True,
    )

    up_got, down_got, crossed = send(to_up, up), send(to_down, down), send(crossing, cross)
    w_got = send(w, other)
    (input_grad,) = stage("s5", [(256, m0, up_got, down_got, crossed)])
    return (input_grad, joined(core, w, w_got).astype(jnp.float32))


def solution(mesh):
    in_specs = (
        P(("row", "rep"), None),
        P(("row", "rep"), None),
        P(("row", "rep"), None),
        P(),
        P("row", "rep", None, None, None, None),
        P("row", "rep", None, None),
        P("row", "rep", None, None),
        P("row", "rep", None),
    )
    out_specs = (P(("row", "rep"), None), P())
    return jax.shard_map(local, mesh=mesh, in_specs=in_specs, out_specs=out_specs, check_vma=False)
```

```python
import functools

import jax
import jax.numpy as jnp
from jax import lax
from jax.experimental import pallas as pl
from jax.experimental.pallas import tpu as pltpu
from jax.sharding import PartitionSpec as P

AXES = ("row", "rep")
X, Y, Z, C = 4, 4, 8, 2


def index_of(x, y, z, c):
    return (z * 2 + x // 2) * 16 + (x % 2) * 8 + y * 2 + c


def pairs(move):
    out = []
    for z in range(Z):
        for x in range(X):
            for y in range(Y):
                for c in range(C):
                    to = move(x, y, z, c)
                    if to is not None:
                        out.append((index_of(x, y, z, c), index_of(to[0] % X, to[1] % Y, to[2] % Z, to[3] % C)))
    return out


def send(value, move):
    return lax.ppermute(value, AXES, pairs(move))


def add(*terms):
    total = terms[0].astype(jnp.float32)
    for term in terms[1:]:
        total = total + term.astype(jnp.float32)
    return total


def narrow(value):
    return value.astype(jnp.bfloat16)


def across(x, y, z, c):
    return (x + 1, y, z, c) if x % 2 == 0 and y < 2 else None


def outward(x, y, z, c):
    return (x, 3 - y, z, c) if x % 2 == 0 and y < 2 else None


def swap(x, y, z, c):
    return (x, 1 - y, z, c) if x % 2 == 0 and y < 2 else None


def swap_rest(x, y, z, c):
    return (x, 5 - y, z, c) if x % 2 == 0 and y >= 2 else None


def across_all(x, y, z, c):
    return (x + 1, y, z, c) if x % 2 == 0 else None


def distant(x, y, z, c):
    return (x, y + 2, z, c) if x % 2 == 1 and y < 2 else None


FIRST = [(4, 1), (2, 1), (6, 1)]
SECOND = [(3, 1), (5, 1), (4, 0), (1, 1), (7, 1)]
THIRD = [(3, 0), (5, 0), (0, 1), (2, 0), (6, 0), (1, 0), (7, 0), (0, 0)]
SLOTS = 96


COUNT = 8
SPARE = 32


def plan_kernel(src_ref, dst_ref, count_ref, order_ref, given_ref, table_ref, passed_ref):
    row = lax.axis_index("row")
    z, xh, core = row // 2, lax.rem(row, 2), lax.rem(lax.axis_index("rep"), 2)
    for i in range(SPARE + 1):
        table_ref[i, COUNT] = 0
    for section in range(4):
        slot = jnp.where(core == section % 2, section // 2, 2 + section // 2)
        live = count_ref[section]

        def step(t, carry):
            d = dst_ref[section, t]
            rel = ((d >> 2) - z) & 7
            half = ((d >> 1) + xh) & 1
            at = jnp.where(t < live, order_ref[rel * 2 + half] * 2 + (d & 1), SPARE)
            n = table_ref[at, COUNT]
            table_ref[at, n & 7] = (section * 24 + t) * 8 + slot * 2 + src_ref[section, t]
            table_ref[at, COUNT] = n + 1
            return carry

        lax.fori_loop(0, 24, step, 0, unroll=True)
    passed_ref[...] = given_ref[...]


def plan(src, dst, count, given):
    order = [0] * 16
    for i, (rel, half) in enumerate(FIRST + SECOND + THIRD):
        order[rel * 2 + half] = i
    smem, vmem = pl.BlockSpec(memory_space=pltpu.SMEM), pl.BlockSpec(memory_space=pltpu.VMEM)
    return pl.pallas_call(
        plan_kernel,
        out_shape=[jax.ShapeDtypeStruct((SPARE + 1, 16), jnp.int32), jax.ShapeDtypeStruct(given.shape, given.dtype)],
        in_specs=[smem] * 4 + [vmem],
        out_specs=[smem, vmem],
        compiler_params=pltpu.CompilerParams(vmem_limit_bytes=10 * 1024 * 1024),
        name="plan",
    )(src, dst, count, jnp.array(order, jnp.int32), given)


def rows_kernel(base, sizes, table_ref, tiles_ref, sources_ref, *rest):
    outs, acc = rest[: len(sizes)], rest[len(sizes)]

    def masked(at, slot, n):
        live = slot < n
        code = jnp.where(live, table_ref[at, slot], 0)
        tile = tiles_ref[code >> 3]
        return jnp.where(live, tile, jnp.zeros_like(tile)), sources_ref[code & 7]

    def pair(at, p, n):
        (left, right), (left2, right2) = masked(at, 2 * p, n), masked(at, 2 * p + 1, n)
        return lax.dot_general(
            jnp.concatenate([left, left2], axis=0),
            jnp.concatenate([right, right2], axis=0),
            (((0,), (0,)), ((), ())),
            preferred_element_type=jnp.float32,
        )

    for g, size in enumerate(sizes):
        first = base + 2 * sum(sizes[:g])

        def blocks(j, carry):
            at = first + 2 * j
            n, n2 = table_ref[at, COUNT], table_ref[at + 1, COUNT]
            acc[0] = pair(at, 0, n)
            acc[1] = pair(at + 1, 0, n2)

            def more(p, c):
                acc[0] += pair(at, p, n)
                acc[1] += pair(at + 1, p, n2)
                return c

            lax.fori_loop(1, (jnp.maximum(n, n2) + 1) // 2, more, 0)
            start = pl.multiple_of(j * 256, 256)
            outs[g][pl.ds(start, 128), :] = acc[0].astype(jnp.bfloat16)
            outs[g][pl.ds(start + 128, 128), :] = acc[1].astype(jnp.bfloat16)
            return carry

        lax.fori_loop(0, size, blocks, 0)


def rows(base, sizes, table, tiles, sources, name):
    smem = pl.BlockSpec(memory_space=pltpu.SMEM)
    vmem = pl.BlockSpec(memory_space=pltpu.VMEM)
    return pl.pallas_call(
        functools.partial(rows_kernel, base, tuple(sizes)),
        out_shape=[jax.ShapeDtypeStruct((256 * size, 512), jnp.bfloat16) for size in sizes],
        in_specs=[smem, vmem, vmem],
        out_specs=[vmem] * len(sizes),
        scratch_shapes=[pltpu.VMEM((2, 128, 512), jnp.float32)],
        compiler_params=pltpu.CompilerParams(vmem_limit_bytes=10 * 1024 * 1024),
        cost_estimate=pl.CostEstimate(flops=sum(sizes) * 400_000_000, bytes_accessed=1_000_000, transcendentals=0),
        name=name,
    )(table, tiles, sources)


def stage_kernel(plans, n_in, n_anchors, *refs):
    ins, outs = refs[:n_in], refs[n_in + n_anchors :]
    for out, segments in zip(outs, plans):
        at = 0
        for count, terms in segments:
            values = [ins[i][pl.ds(start, count), :].astype(jnp.float32) for i, start in terms]
            while len(values) > 1:
                values = [sum(values[i : i + 2]) for i in range(0, len(values), 2)]
            out[pl.ds(at, count), :] = values[0].astype(out.dtype)
            at += count


def collect_kernel(plans, n_in, pieces, *refs):
    stage_kernel(plans, n_in, pieces, *refs[:-1])
    y = lax.rem(lax.axis_index("rep") // 2, 4)
    for step in range(pieces):
        owner = y ^ step
        start = pl.multiple_of((owner & 1) * 128 + (owner >> 1) * 64, 64)
        refs[-1][pl.ds(start, 64), :] = refs[n_in + step][...]


def stage(name, *outputs, anchors=(), collect=False):
    arrays, plans, shapes = [], [], []
    for segments in outputs:
        planned = []
        for count, *terms in segments:
            numbered = []
            for term in terms:
                value, start = term if isinstance(term, tuple) else (term, 0)
                place = next((i for i, known in enumerate(arrays) if known is value), None)
                if place is None:
                    place = len(arrays)
                    arrays.append(value)
                numbered.append((place, start))
            planned.append((count, tuple(numbered)))
        plans.append(tuple(planned))
        shapes.append(jax.ShapeDtypeStruct((sum(count for count, _ in planned), 512), jnp.bfloat16))
    if collect:
        shapes.append(jax.ShapeDtypeStruct((256, 512), jnp.bfloat16))
    vmem, anywhere = pl.BlockSpec(memory_space=pltpu.VMEM), pl.BlockSpec(memory_space=pl.ANY)
    return pl.pallas_call(
        functools.partial(collect_kernel if collect else stage_kernel, tuple(plans), len(arrays), len(anchors)),
        out_shape=shapes,
        in_specs=[vmem] * len(arrays) + [anywhere if anchor.dtype == jnp.int32 else vmem for anchor in anchors],
        out_specs=[vmem] * len(shapes),
        compiler_params=pltpu.CompilerParams(vmem_limit_bytes=6 * 1024 * 1024),
        cost_estimate=pl.CostEstimate(flops=1000, bytes_accessed=1000, transcendentals=0),
        name=name,
    )(*arrays, *anchors)


def up(x, y, z, c):
    return (x, y, z + 1, c)


def down(x, y, z, c):
    return (x, y, z - 1, c)


def halves(value, bit):
    rows = value.shape[0] // 2
    kept = lax.dynamic_slice_in_dim(value, bit * rows, rows, 0)
    return kept, narrow(lax.dynamic_slice_in_dim(value, (1 - bit) * rows, rows, 0))


def joined(bit, value, got):
    return jnp.concatenate([jnp.where(bit == 0, value, got), jnp.where(bit == 0, got, value)])


def later(name, anchor, *terms):
    return stage(name, [(terms[0].shape[0], *terms)], anchors=(anchor,))[0]


def flipped(axis, step):
    def move(x, y, z, c):
        at = {"x": x, "y": y, "z": z, "c": c}
        at[axis] ^= step
        return at["x"], at["y"], at["z"], at["c"]

    return move


def local(grad_out, relu_mask, aggregated, weight, tile_values, tile_src, tile_dst, tile_count):
    rep = lax.axis_index("rep")
    x_lo, y, core = rep // 8, (rep // 2) % 4, rep % 2
    other, cross = flipped("c", 1), flipped("x", 2)
    tiles = tile_values.reshape(SLOTS, 128, 128)

    masked = jnp.where(relu_mask != 0, grad_out, jnp.zeros_like(grad_out))
    node_grad = lax.dot_general(
        masked, weight, (((1,), (1,)), ((), ())), preferred_element_type=jnp.float32
    ).astype(jnp.bfloat16)
    w = lax.dot_general(aggregated, masked, (((0,), (0,)), ((), ())), preferred_element_type=jnp.float32)
    kept, given = halves(w, core)
    table, given = plan(tile_src[0, 0], tile_dst[0, 0], tile_count[0, 0], given)
    by_x, by_y, swapped = send(node_grad, across), send(node_grad, outward), send(node_grad, swap)
    w = add(kept, send(given, other))
    kept, given = halves(w, y % 2)
    onward = jnp.where(y < 2, swapped, by_y)
    by_x2, by_far, by_swap = send(onward, across_all), send(by_x, distant), send(by_y, swap_rest)
    w = add(kept, send(given, flipped("y", 1)))
    first = jnp.where(x_lo == 0, jnp.where(y < 2, node_grad, by_y), jnp.where(y < 2, by_x, by_x2))
    second = jnp.where(x_lo == 0, jnp.where(y < 2, swapped, by_swap), jnp.where(y < 2, by_x2, by_far))
    flip = jnp.logical_or(y == 1, y == 2)
    even, odd = jnp.where(flip, second, first), jnp.where(flip, first, second)

    even2, odd2 = send(even, other), send(odd, other)
    sources, w = stage("s0", [(256, even), (256, odd), (256, even2), (256, odd2)], [(128, narrow(w))])
    sources = sources.reshape(8, 128, 512)

    w_got = send(w, flipped("z", 1))
    t4, t2, t6 = rows(0, [1, 1, 1], table, tiles, sources, "rows_first")
    x4, up_got, down_got = send(t4, cross), send(t2, up), send(t6, down)
    kept, given = halves(later("v1", t4, w, w_got), y // 2)
    w_got = send(given, flipped("y", 2))
    t35, m4, t1, t7 = rows(6, [2, 1, 1, 1], table, tiles, sources, "rows_second")
    to_up, to_down, t35, w = stage(
        "s1",
        [(256, t1, up_got), (128, m4, x4)],
        [(256, t7, down_got), (128, (m4, 128), (x4, 128))],
        [(512, t35)],
        [(64, kept, w_got)],
    )

    up_t, down_t, x35 = send(to_up, up), send(to_down, down), send(t35, cross)
    w = narrow(add(w, send(w, flipped("z", 2))))
    w_got = send(w, flipped("z", 4))
    m3, m5, t0, m2, m6, m1, m7, m0 = rows(16, [1] * 8, table, tiles, sources, "rows_third")
    to_up, to_down, crossing, w = stage(
        "s2",
        [(128, m3, x35, (up_t, 256)), (128, (m3, 128), (x35, 128))],
        [(128, m5, (x35, 256)), (128, (m5, 128), (x35, 384), (down_t, 256))],
        [(256, t0, up_t, down_t)],
        [(64, w, w_got)],
    )

    up_got, down_got = send(to_up, up), send(to_down, down)
    crossed = send(crossing, cross)
    w_got = [send(w, flipped("x", step)) for step in (1, 2, 3)]
    to_up, to_down, w = stage("s3", [(256, m2, up_got)], [(256, m6, down_got)], [(64, w, *w_got)])

    up_got, down_got = send(to_up, up), send(to_down, down)
    w_got = [send(w, flipped("y", step)) for step in (1, 2, 3)]
    to_up, to_down, w = stage(
        "s4",
        [(256, m1, up_got)],
        [(256, m7, down_got)],
        anchors=(w, *w_got),
        collect=True,
    )

    up_got, down_got = send(to_up, up), send(to_down, down)
    w_got = send(w, other)
    (input_grad,) = stage("s5", [(256, m0, up_got, down_got, crossed)])
    return (input_grad, joined(core, w, w_got).astype(jnp.float32))


def solution(mesh):
    in_specs = (
        P(("row", "rep"), None),
        P(("row", "rep"), None),
        P(("row", "rep"), None),
        P(),
        P("row", "rep", None, None, None, None),
        P("row", "rep", None, None),
        P("row", "rep", None, None),
        P("row", "rep", None),
    )
    out_specs = (P(("row", "rep"), None), P())
    return jax.shard_map(local, mesh=mesh, in_specs=in_specs, out_specs=out_specs, check_vma=False)
```
